128 devices in a mesh: row: 8 (over y_lo, x), col: 16 (over z, y_hi, core).
Axes of the slice: x: 4, y: 4 (y_hi: 2, y_lo: 2; y = y_hi * 2 + y_lo), z: 4, core: 2. Of those that a mesh axis runs over, the one named last changes fastest.
Arguments:
- hidden_in: bfloat16 [2048, 8192], P('col', 'row'), may hold values from -130 to 130
- norm_gain: float32 [8192], P('row'), may hold values from 0.5 to 1.5
- w_query: bfloat16 [8192, 8192], P('row', 'col'), may hold values from -0.0625 to 0.0625
- scale_query: float32 [64, 64], P('row', 'col'), may hold values from 0.35 to 2.8
- bias_query: float32 [8192], P('col'), may hold values from -14 to 14
- w_keyval: bfloat16 [8192, 2048], P('row'), may hold values from -0.0625 to 0.0625
- scale_keyval: float32 [64, 16], P('row'), may hold values from 0.35 to 2.8
- bias_keyval: float32 [2048], replicated, may hold values from -3 to 3
- w_out: bfloat16 [8192, 8192], P('col', 'row'), may hold values from -0.0625 to 0.0625
- scale_out: float32 [64, 64], P('col', 'row'), may hold values from 0.35 to 2.8
- cache_keyval: bfloat16 [2, 8192, 1024], P(None, 'row'), may hold values from -14 to 14
- span_offset: int32 [1], replicated, may hold values from 2048 to 8192
Outputs:
- hidden_out: bfloat16 [2048, 8192], P('col', 'row')
The draws below stay inside these ranges and needn't reach their ends.
All inputs are finite; a program needn't handle non-finite values.
Results may differ from the reference program's by a relative error of at most 0.033.
Values may be sent and summed in bfloat16 or wider, within the bound.
No kernel may reach another device: no remote copies, remote signals or barrier semaphores. Data moves between devices by JAX's collectives and lax.ppermute only.
A program may use at most 192 MiB of HBM per device.

```python
import math
import jax
import jax.numpy as jnp
from jax import lax

D = 8192
H = 64
KVH = 8
HD = 128
QB = 128
QW = 8192
KW = 1024
TOKENS = 2048
CACHE = 8192


def draw_hidden_in(key, part):
    subkeys = jax.random.split(key, 3)
    column_pos = jnp.arange(D, dtype=jnp.float32) / D
    roughness = jnp.exp(jax.random.uniform(subkeys[1], (D,), jnp.float32, jnp.log(0.5), 0.0))
    column_scale = 0.3 * jnp.exp(jnp.log(10.0) * column_pos) * roughness
    row_scale = jnp.exp(jax.random.uniform(subkeys[2], (TOKENS, 1), jnp.float32, 0.0, jnp.log(10.0)))
    basis = jax.random.truncated_normal(subkeys[0], -4.0, 4.0, (TOKENS, D), jnp.float32)
    return (basis * column_scale[None, :] * row_scale).astype(jnp.bfloat16)


def draw_bias_query(key, part):
    subkeys = jax.random.split(key, 1)
    basis = 0.5 * jax.random.truncated_normal(subkeys[0], -4.0, 4.0, (H, HD), jnp.float32)
    return basis.reshape(H * HD)


def draw_cache_keyval(key, part):
    subkeys = jax.random.split(key, 2)
    kind_index = jnp.arange(2)[:, None, None]
    value_shift = 0.7 * jax.random.truncated_normal(subkeys[1], -4.0, 4.0, (1, 1, KW), jnp.float32)
    noise_part = jax.random.truncated_normal(subkeys[0], -4.0, 4.0, (2, CACHE, KW), jnp.float32)
    result = noise_part + jnp.where(kind_index == 1, value_shift, 0.0)
    return result.astype(jnp.bfloat16)


def block_levels(key, dims, shards, smallest, top_value):
    level = 1.0
    for axis_at, parts in shards:
        heights = jax.random.uniform(jax.random.fold_in(jax.random.fold_in(key, 6), axis_at), (parts,), jnp.float32, smallest / len(shards), top_value / len(shards))
        level = level * jnp.repeat(jnp.exp(heights), dims[axis_at] // parts).reshape((-1,) + (1,) * (len(dims) - 1 - axis_at))
    return level


def centred(rng, extent, spread, bound, pieces=(), kind=jnp.bfloat16):
    entries = spread * jax.random.normal(rng, extent, jnp.float32)
    if pieces:
        entries = entries * block_levels(rng, extent, pieces, -0.22, 0.18)
    return jnp.clip(entries, -bound, bound).astype(kind)


def setup_inputs(seed: int = 0) -> dict:
    key_of = jax.random.split(jax.random.key(seed), 13)
    hidden_in = draw_hidden_in(jax.random.fold_in(key_of[12], 71), 0)
    norm_gain = jnp.clip(1.0 + 0.1 * jax.random.normal(key_of[1], (D,), jnp.float32), 0.5, 1.5)
    w_query = centred(key_of[2], (D, QW), D ** -0.5, 0.0625, ((0, 8), (1, 16)))
    scale_query = jnp.clip(jnp.exp(math.log(2.8) - 2.0794415 * jax.random.uniform(key_of[3], (D // QB, QW // QB), jnp.float32) ** block_levels(key_of[3], (D // QB, QW // QB), ((0, 8), (1, 16)), -0.2, 0.2)), 0.35, 2.8)
    bias_query = draw_bias_query(jax.random.fold_in(key_of[12], 71), 0)
    w_keyval = centred(key_of[5], (D, 2 * KW), D ** -0.5, 0.0625, ((0, 8),))
    scale_keyval = jnp.clip(jnp.exp(math.log(2.8) - 2.0794415 * jax.random.uniform(key_of[6], (D // QB, 2 * KW // QB), jnp.float32) ** block_levels(key_of[6], (D // QB, 2 * KW // QB), ((0, 8),), -0.2, 0.2)), 0.35, 2.8)
    bias_keyval = centred(key_of[7], (2 * KW,), 0.5, 3.0, (), jnp.float32)
    w_out = centred(key_of[8], (QW, D), QW ** -0.5, 0.0625, ((0, 16), (1, 8)))
    scale_out = jnp.clip(jnp.exp(math.log(2.8) - 2.0794415 * jax.random.uniform(key_of[9], (QW // QB, D // QB), jnp.float32) ** block_levels(key_of[9], (QW // QB, D // QB), ((0, 16), (1, 8)), -0.2, 0.2)), 0.35, 2.8)
    cache_keyval = draw_cache_keyval(jax.random.fold_in(key_of[12], 71), 0)
    span_offset = jax.random.randint(key_of[11], (1,), CACHE // 4, CACHE + 1).astype(jnp.int32)
    return {"hidden_in": hidden_in, "norm_gain": norm_gain, "w_query": w_query, "scale_query": scale_query, "bias_query": bias_query, "w_keyval": w_keyval, "scale_keyval": scale_keyval, "bias_keyval": bias_keyval, "w_out": w_out, "scale_out": scale_out, "cache_keyval": cache_keyval, "span_offset": span_offset}


EPSILON = 1e-06
ROPE_BASE = 1000000.0
MASKED = -1e+30

def dequantize(weight, block_scale):
    expanded = jnp.repeat(jnp.repeat(block_scale, QB, axis=0), QB, axis=1)
    return (weight.astype(jnp.float32) * expanded).astype(jnp.bfloat16)

def rotate(vectors, positions):
    half_dim = HD // 2
    inverse = ROPE_BASE ** (-(2.0 * jnp.arange(half_dim, dtype=jnp.float32)) / HD)
    angles = positions[:, None] * inverse[None, :]
    cosine = jnp.cos(angles)[:, None, :]
    sine_part = jnp.sin(angles)[:, None, :]
    first_half = vectors[..., :half_dim]
    second = vectors[..., half_dim:]
    return jnp.concatenate([first_half * cosine - second * sine_part, second * cosine + first_half * sine_part], axis=-1)

def block_scores(queries, key_block, key_index, query_index, offset, cache_len):
    scores = jnp.einsum('thd,kd->htk', queries.astype(jnp.float32), key_block.astype(jnp.float32)) * (1.0 / math.sqrt(HD))
    earlier = (key_index < cache_len)[None, :]
    allowed = jnp.where(earlier, (key_index < offset)[None, :], (key_index - cache_len)[None, :] <= query_index[:, None])
    return jnp.where(allowed[None, :, :], scores, MASKED)

def softmax_stats(queries, key_rows, key_index, query_index, offset, cache_len, block_len):
    key_blocks = key_rows.reshape(-1, block_len, key_rows.shape[-1])
    index_blocks = key_index.reshape(-1, block_len)

    def advance(running, block_item):
        row_peak, row_total = running
        scores = block_scores(queries, block_item[0], block_item[1], query_index, offset, cache_len)
        new_peak = jnp.maximum(row_peak, lax.optimization_barrier(jnp.max(scores, axis=2)))
        weights = jnp.where(scores > 0.5 * MASKED, jnp.exp(scores - new_peak[:, :, None]), 0.0)
        row_total = row_total * jnp.exp(row_peak - new_peak) + lax.optimization_barrier(jnp.sum(weights, axis=2))
        return ((new_peak, row_total), None)
    start_state = (jnp.full((queries.shape[1], queries.shape[0]), MASKED, jnp.float32), jnp.zeros((queries.shape[1], queries.shape[0]), jnp.float32))
    return lax.scan(advance, start_state, (key_blocks, index_blocks))[0]

def softmax_output(queries, key_rows, value_rows, key_index, query_index, offset, cache_len, block_len, row_peak, row_total):
    key_blocks = key_rows.reshape(-1, block_len, key_rows.shape[-1])
    value_blocks = value_rows.reshape(-1, block_len, value_rows.shape[-1])
    index_blocks = key_index.reshape(-1, block_len)

    def advance(summed, block_item):
        scores = block_scores(queries, block_item[0], block_item[2], query_index, offset, cache_len)
        weights = (jnp.exp(scores - row_peak[:, :, None]) / row_total[:, :, None]).astype(jnp.bfloat16)
        return (summed + jnp.einsum('htk,kd->thd', weights.astype(jnp.float32), block_item[1].astype(jnp.float32)), None)
    start_state = jnp.zeros((queries.shape[0], queries.shape[1], HD), jnp.float32)
    return lax.scan(advance, start_state, (key_blocks, value_blocks, index_blocks))[0]

def reference(hidden_in, norm_gain, w_query, scale_query, bias_query, w_keyval, scale_keyval, bias_keyval, w_out, scale_out, cache_keyval, span_offset):
    widened = hidden_in.astype(jnp.float32)
    norm_ratio = lax.rsqrt(lax.optimization_barrier(jnp.mean(widened * widened, axis=1, keepdims=True)) + EPSILON)
    normed = (widened * norm_ratio * norm_gain[None, :]).astype(jnp.bfloat16)
    offset = span_offset[0]
    query_index = jnp.arange(TOKENS, dtype=jnp.int32)
    positions = (offset + query_index).astype(jnp.float32)
    query_raw = jnp.dot(normed, dequantize(w_query, scale_query), preferred_element_type=jnp.float32) + bias_query[None, :]
    queries_all = rotate(query_raw.reshape(TOKENS, H, HD), positions).astype(jnp.bfloat16)
    keyval_raw = jnp.dot(normed, dequantize(w_keyval, scale_keyval), preferred_element_type=jnp.float32) + bias_keyval[None, :]
    span_keys = rotate(keyval_raw[:, :KW].reshape(TOKENS, KVH, HD), positions).astype(jnp.bfloat16)
    span_values = keyval_raw[:, KW:].reshape(TOKENS, KVH, HD).astype(jnp.bfloat16)
    key_index = jnp.arange(CACHE + TOKENS, dtype=jnp.int32)
    group_size = H // KVH

    def one_head(kv_index):
        queries = lax.dynamic_slice_in_dim(queries_all, kv_index * group_size, group_size, 1)
        cached_keys = lax.dynamic_slice_in_dim(cache_keyval[0], kv_index * HD, HD, 1)
        cached_values = lax.dynamic_slice_in_dim(cache_keyval[1], kv_index * HD, HD, 1)
        key_rows = jnp.concatenate([cached_keys, lax.dynamic_index_in_dim(span_keys, kv_index, 1, keepdims=False)], axis=0)
        value_rows = jnp.concatenate([cached_values, lax.dynamic_index_in_dim(span_values, kv_index, 1, keepdims=False)], axis=0)
        row_peak, row_total = softmax_stats(queries, key_rows, key_index, query_index, offset, CACHE, TOKENS)
        return softmax_output(queries, key_rows, value_rows, key_index, query_index, offset, CACHE, TOKENS, row_peak, row_total)
    head_outputs = lax.map(one_head, jnp.arange(KVH, dtype=jnp.int32))
    attended = jnp.transpose(head_outputs, (1, 0, 2, 3)).reshape(TOKENS, QW).astype(jnp.bfloat16)
    mixed_out = jnp.dot(attended, dequantize(w_out, scale_out), preferred_element_type=jnp.float32)
    return mixed_out.astype(jnp.bfloat16)
```

```python
import functools
import math

import jax
import jax.numpy as jnp
from jax import lax
from jax.experimental import pallas as pl
from jax.experimental.pallas import tpu as pltpu
from jax.sharding import Mesh
from jax.sharding import PartitionSpec as P

D = 8192
H = 64
KVH = 8
HD = 128
QB = 128
TOK = 128
GROUP = 8
SLOTS = 1024
HALF = 512

EPSILON = 1e-06
ROPE_BASE = 1000000.0
LOWEST = -1e30
ROW = ("ylo", "x")
COL = ("z", "yhi")
QSCALE = math.log2(math.e) / math.sqrt(HD)
PIECES = (0, 4, 1, 5, 3, 7, 2, 6)
VMEM = 48 * 2**20


def expand(block_scale):
    return jnp.repeat(jnp.repeat(block_scale, QB, axis=0), QB, axis=1)


def swap_cores(array):
    return lax.ppermute(array, "core", [(0, 1), (1, 0)])


def along(array, axis, size, distance):
    return lax.ppermute(array, axis, [(i, i ^ distance) for i in range(size)])


def gather(array, axes):
    return lax.all_to_all(
        jnp.broadcast_to(array[None], (GROUP,) + array.shape), axes, 0, 0, tiled=True
    )


def gather_cache(cache_keyval, head, core):
    mine = lax.dynamic_slice(cache_keyval, (0, core * HALF, head * HD), (2, HALF, HD))
    pair = jnp.stack([mine, along(mine, "ylo", 2, 1)])
    first = along(pair, "x", 4, 1)
    third = along(pair, "x", 4, 3)
    second_a = along(first[0:1], "x", 4, 3)
    second_b = along(third[1:2], "x", 4, 1)
    own = jnp.concatenate([pair, first, third, second_a, second_b], axis=0)
    return own, swap_cores(own)


def finish_kernel(parts_ref, ratio_ref, bias_ref, cos_ref, sin_ref, q_ref, kv_ref):
    ratio = ratio_ref[...]
    cosine = cos_ref[...]
    sine = sin_ref[...]
    for column in range(GROUP + 2):
        lanes = slice(column * HD, (column + 1) * HD)
        total = parts_ref[0, :, lanes].astype(jnp.float32)
        for part in range(1, GROUP):
            total = total + parts_ref[part, :, lanes].astype(jnp.float32)
        total = total * ratio + bias_ref[:, lanes]
        if column <= GROUP:
            total = total * cosine + pltpu.roll(total, HD // 2, 1) * sine
        if column < GROUP:
            q_ref[column] = (total * QSCALE).astype(jnp.bfloat16)
        else:
            kv_ref[column - GROUP] = total.astype(jnp.bfloat16)


def finish(parts, ratio, bias, cosine, sine):
    return pl.pallas_call(
        finish_kernel,
        out_shape=(
            jax.ShapeDtypeStruct((GROUP, TOK, HD), jnp.bfloat16),
            jax.ShapeDtypeStruct((2, TOK, HD), jnp.bfloat16),
        ),
        in_specs=[pl.BlockSpec(memory_space=pltpu.VMEM)] * 5,
        out_specs=(pl.BlockSpec(memory_space=pltpu.VMEM),) * 2,
        compiler_params=pltpu.CompilerParams(vmem_limit_bytes=VMEM),
    )(parts, ratio, bias, cosine, sine)


def with_ones(values):
    return jnp.concatenate([values, jnp.ones(values.shape, values.dtype)], axis=1)


def absorb(rows, query, keys, values, masks, peak_ref, acc_ref):
    scores = []
    for key, mask in zip(keys, masks, strict=True):
        score = lax.dot_general(
            query, key, (((1,), (1,)), ((), ())), preferred_element_type=jnp.float32
        )
        scores.append(score if mask is None else jnp.where(mask, score, LOWEST))
    old = peak_ref[rows, :]
    new = old
    for score in scores:
        new = jnp.maximum(new, jnp.max(score, axis=1, keepdims=True))
    fresh = None
    for score, value in zip(scores, values, strict=True):
        weights = jnp.exp2(score - new).astype(jnp.bfloat16)
        part = jnp.dot(weights, value, preferred_element_type=jnp.float32)
        fresh = part if fresh is None else fresh + part
    acc_ref[rows, :] = acc_ref[rows, :] * jnp.exp2(old - new) + fresh
    peak_ref[rows, :] = new


CHUNK = 256
ROWS = GROUP * TOK


def cache_kernel(place_ref, q_ref, own_ref, peer_ref, acc_ref, peak_ref):
    offset = place_ref[0]
    core = place_ref[1]
    acc_ref[...] = jnp.zeros_like(acc_ref)
    peak_ref[...] = jnp.full_like(peak_ref, LOWEST)

    def piece(index, carry):
        base = place_ref[2 + index] * SLOTS
        own_base = base + core * HALF
        peer_base = base + (1 - core) * HALF

        def step(masked):
            keys = [own_ref[index, 0], peer_ref[index, 0]]
            values = [with_ones(own_ref[index, 1]), with_ones(peer_ref[index, 1])]
            masks = [None, None]
            if masked:
                slot = lax.broadcasted_iota(jnp.int32, (CHUNK, HALF), 1)
                masks = [slot + own_base < offset, slot + peer_base < offset]
            for start in range(0, ROWS, CHUNK):
                rows = slice(start, start + CHUNK)
                absorb(rows, q_ref[rows, :], keys, values, masks, peak_ref, acc_ref)

        @pl.when(base + SLOTS <= offset)
        def _():
            step(False)

        @pl.when((base < offset) & (base + SLOTS > offset))
        def _():
            step(True)

        return carry

    lax.fori_loop(0, GROUP, piece, 0)


def attend_cache(place, queries, own, peer):
    return pl.pallas_call(
        cache_kernel,
        out_shape=(
            jax.ShapeDtypeStruct((ROWS, 2 * HD), jnp.float32),
            jax.ShapeDtypeStruct((ROWS, 1), jnp.float32),
        ),
        in_specs=[pl.BlockSpec(memory_space=pltpu.SMEM)]
        + [pl.BlockSpec(memory_space=pltpu.VMEM)] * 3,
        out_specs=(pl.BlockSpec(memory_space=pltpu.VMEM),) * 2,
        compiler_params=pltpu.CompilerParams(vmem_limit_bytes=VMEM),
        cost_estimate=pl.CostEstimate(
            flops=16 * 2**30, bytes_accessed=8 * 2**20, transcendentals=2**23
        ),
    )(place, queries, own, peer)


def span_kernel(place_ref, q_ref, own_ref, peer_ref, acc_in, peak_in, out_ref, acc_ref, peak_ref):
    core = place_ref[1]
    mine = 2 * place_ref[2] + core
    acc_ref[...] = acc_in[...]
    peak_ref[...] = peak_in[...]
    blocks = 4
    width = blocks * TOK
    for start in range(0, GROUP, blocks):
        for ref, other in ((own_ref, core), (peer_ref, 1 - core)):
            first = 2 * start + other
            last = first + 2 * (blocks - 1)

            def step(masked, ref=ref, start=start, first=first):
                key = ref[start : start + blocks, 0].reshape(width, HD)
                value = with_ones(ref[start : start + blocks, 1].reshape(width, HD))
                mask = None
                if masked:
                    lane = lax.broadcasted_iota(jnp.int32, (CHUNK, width), 1)
                    token = (first + 2 * (lane // TOK)) * TOK + lane % TOK
                    row = lax.broadcasted_iota(jnp.int32, (CHUNK, width), 0)
                    mask = token <= mine * TOK + row % TOK
                for begin in range(0, ROWS, CHUNK):
                    rows = slice(begin, begin + CHUNK)
                    absorb(rows, q_ref[rows, :], [key], [value], [mask], peak_ref, acc_ref)

            @pl.when(last < mine)
            def _(step=step):
                step(False)

            @pl.when((first <= mine) & (last >= mine))
            def _(step=step):
                step(True)

    for head in range(GROUP):
        rows = slice(head * TOK, (head + 1) * TOK)
        out_ref[:, head * HD : (head + 1) * HD] = (
            acc_ref[rows, :HD] / acc_ref[rows, HD:]
        ).astype(jnp.bfloat16)


def attend_span(place, queries, own, peer, acc, peak):
    return pl.pallas_call(
        span_kernel,
        out_shape=jax.ShapeDtypeStruct((TOK, GROUP * HD), jnp.bfloat16),
        in_specs=[pl.BlockSpec(memory_space=pltpu.SMEM)]
        + [pl.BlockSpec(memory_space=pltpu.VMEM)] * 5,
        out_specs=pl.BlockSpec(memory_space=pltpu.VMEM),
        scratch_shapes=[
            pltpu.VMEM((ROWS, 2 * HD), jnp.float32),
            pltpu.VMEM((ROWS, 1), jnp.float32),
        ],
        compiler_params=pltpu.CompilerParams(vmem_limit_bytes=VMEM),
        cost_estimate=pl.CostEstimate(
            flops=4 * 2**30, bytes_accessed=4 * 2**20, transcendentals=2**21
        ),
    )(place, queries, own, peer, acc, peak)


def body(
    hidden_in,
    norm_gain,
    w_query,
    scale_query,
    bias_query,
    w_keyval,
    scale_keyval,
    bias_keyval,
    w_out,
    scale_out,
    cache_keyval,
    span_offset,
):
    row = lax.axis_index(ROW)
    head = lax.axis_index(COL)
    core = lax.axis_index("core")
    offset = span_offset[0]

    gathered = gather(hidden_in, COL).reshape(GROUP * TOK, -1)

    widened = hidden_in.astype(jnp.float32)
    squares = lax.psum(jnp.sum(widened * widened, axis=1), ROW)
    ratio = lax.ppermute(
        lax.rsqrt(squares / D + EPSILON),
        ROW + COL,
        [(r * GROUP + b, b * GROUP + r) for r in range(GROUP) for b in range(GROUP)],
    )

    query_own = (
        w_query.astype(jnp.float32) * expand(scale_query) * norm_gain[:, None]
    ).astype(jnp.bfloat16)
    query_peer = swap_cores(query_own)
    bias_peer = swap_cores(bias_query)
    keyval = []
    bias = [bias_query, bias_peer]
    for kind in range(2):
        start = kind * KVH + head
        weight = lax.dynamic_slice_in_dim(w_keyval, start * HD, HD, 1)
        scale = lax.dynamic_slice_in_dim(scale_keyval, start, 1, 1)
        keyval.append(
            (weight.astype(jnp.float32) * expand(scale) * norm_gain[:, None]).astype(jnp.bfloat16)
        )
        bias.append(lax.dynamic_slice_in_dim(bias_keyval, start * HD, HD, 0))
    weights = jnp.concatenate([query_own, query_peer] + keyval, axis=1)
    bias = jnp.concatenate(bias)[None, :]

    out_own = (w_out.astype(jnp.float32) * expand(scale_out)).astype(jnp.bfloat16)
    out_weight = jnp.concatenate([out_own, swap_cores(out_own)], axis=0)

    cache_own, cache_peer = gather_cache(cache_keyval, head, core)

    token = (2 * row + core) * TOK + jnp.arange(TOK, dtype=jnp.int32)
    positions = (offset + token).astype(jnp.float32)
    inverse = ROPE_BASE ** (-(2.0 * jnp.arange(HD // 2, dtype=jnp.float32)) / HD)
    angles = positions[:, None] * inverse[None, :]
    cosine = jnp.cos(angles)
    sine = jnp.sin(angles)
    cosine = jnp.concatenate([cosine, cosine], axis=1)
    sine = jnp.concatenate([-sine, sine], axis=1)

    projected = jnp.dot(gathered, weights, preferred_element_type=jnp.float32).astype(jnp.bfloat16)
    parts = lax.all_to_all(projected.reshape(GROUP, TOK, -1), ROW, 0, 0, tiled=True)
    queries, own_kv = finish(parts, ratio[:, None], bias, cosine, sine)
    queries = queries.reshape(ROWS, HD)

    span_own = gather(own_kv, ROW)
    span_peer = swap_cores(span_own)

    order = jnp.array(PIECES, jnp.int32) ^ row
    place = jnp.concatenate([jnp.stack([offset, core]), order]).astype(jnp.int32)
    acc, peak = attend_cache(place, queries, cache_own, cache_peer)
    attended = attend_span(place, queries, span_own, span_peer, acc, peak)

    everyone = gather(attended, ROW).reshape(GROUP * TOK, -1)
    mixed = jnp.dot(everyone, out_weight, preferred_element_type=jnp.float32).astype(jnp.bfloat16)
    shares = lax.all_to_all(mixed.reshape(GROUP, TOK, -1), COL, 0, 0, tiled=True)
    return jnp.sum(shares.astype(jnp.float32), axis=0).astype(jnp.bfloat16)


def solution(mesh):
    fine = Mesh(mesh.devices.reshape(2, 4, 4, 2, 2), ("ylo", "x", "z", "yhi", "core"))
    row = ("ylo", "x")
    col = ("z", "yhi", "core")
    return jax.shard_map(
        body,
        mesh=fine,
        in_specs=(
            P(col, row),
            P(row),
            P(row, col),
            P(row, col),
            P(col),
            P(row, None),
            P(row, None),
            P(),
            P(col, row),
            P(col, row),
            P(None, row, None),
            P(),
        ),
        out_specs=P(col, row),
        check_vma=False,
    )
```

```python
import functools
import math

import jax
import jax.numpy as jnp
from jax import lax
from jax.experimental import pallas as pl
from jax.experimental.pallas import tpu as pltpu
from jax.sharding import Mesh
from jax.sharding import PartitionSpec as P

D = 8192
H = 64
KVH = 8
HD = 128
QB = 128
TOK = 128
GROUP = 8
SLOTS = 1024
HALF = 512

EPSILON = 1e-06
ROPE_BASE = 1000000.0
LOWEST = -1e30
ROW = ("ylo", "x")
COL = ("z", "yhi")
QSCALE = math.log2(math.e) / math.sqrt(HD)
WIDE = 640
SQUARES = 2 * WIDE
PART = 64
NEAR = (0, 4, 3, 7)
FAR = (1, 5, 2, 6)
MEMBERS = ((0, 3, 4, 7), (1, 2, 5, 6))
VMEM = 48 * 2**20


def expand(block_scale):
    return jnp.repeat(jnp.repeat(block_scale, QB, axis=0), QB, axis=1)


def swap_cores(array):
    return lax.ppermute(array, "core", [(0, 1), (1, 0)])


def along(array, axis, size, distance):
    return lax.ppermute(array, axis, [(i, i ^ distance) for i in range(size)])


def beside(array):
    return along(array, "x", 4, 1)


def exchange(array, axes, groups=None):
    return lax.all_to_all(array, axes, 0, 0, tiled=True, axis_index_groups=groups)


def copies(array, count):
    return jnp.broadcast_to(array[None], (count,) + array.shape)


def in_vmem(count):
    return [pl.BlockSpec(memory_space=pltpu.VMEM)] * count


def place_of(block):
    return (block, 0) if block < 4 else (7 - block, PART)


def project_kernel(x_ref, own_ref, own_x_ref, peer_ref, peer_x_ref, out_ref):
    rows = GROUP * PART
    x = x_ref[...].reshape(rows, 2 * SLOTS)
    for start, near, far in ((0, own_ref, own_x_ref), (WIDE, peer_ref, peer_x_ref)):
        total = jnp.dot(x[:, :SLOTS], near[...], preferred_element_type=jnp.float32)
        total = total + jnp.dot(x[:, SLOTS:], far[...], preferred_element_type=jnp.float32)
        total = total.astype(jnp.bfloat16)
        for block in range(GROUP):
            member, row = place_of(block)
            out_ref[member, row : row + PART, start : start + WIDE] = total[
                block * PART : (block + 1) * PART
            ]
    for block in range(GROUP):
        member, row = place_of(block)
        wide = x_ref[block].astype(jnp.float32)
        squares = jnp.sum(wide * wide, axis=1, keepdims=True)
        high = squares.astype(jnp.bfloat16).astype(jnp.float32)
        lane = lax.broadcasted_iota(jnp.int32, (PART, HD), 1)
        both = jnp.where(lane < HD // 2, high, squares - high)
        out_ref[member, row : row + PART, SQUARES:] = both.astype(jnp.bfloat16)


def project(x, *weights):
    return pl.pallas_call(
        project_kernel,
        out_shape=jax.ShapeDtypeStruct((4, TOK, SQUARES + HD), jnp.bfloat16),
        in_specs=in_vmem(5),
        out_specs=pl.BlockSpec(memory_space=pltpu.VMEM),
        compiler_params=pltpu.CompilerParams(vmem_limit_bytes=VMEM),
        cost_estimate=pl.CostEstimate(
            flops=3 * 2**30, bytes_accessed=9 * 2**20, transcendentals=0
        ),
    )(x, *weights)


def finish_kernel(core_ref, parts_ref, bias_ref, cos_ref, sin_ref, q_ref, kv_ref):
    core = core_ref[0]
    cosine = cos_ref[...]
    sine = sin_ref[...]

    def summed(start):
        total = parts_ref[0, :, start : start + HD].astype(jnp.float32)
        for part in range(1, 4):
            total = total + parts_ref[part, :, start : start + HD].astype(jnp.float32)
        return total

    squares = summed(SQUARES)
    ratio = lax.rsqrt((squares[:, :1] + squares[:, HD // 2 : HD // 2 + 1]) / D + EPSILON)
    for side in range(2):
        for column in range(5):
            start = side * WIDE + column * HD
            total = summed(start) * ratio + bias_ref[:, start : start + HD]
            turned = total * cosine + pltpu.roll(total, HD // 2, 1) * sine
            if column < 4:
                turned = (turned * QSCALE).astype(jnp.bfloat16)
                q_ref[0, side * 4 + column] = turned[:PART]
                q_ref[1, side * 4 + column] = turned[PART:]
            else:
                kind = core if side == 0 else 1 - core
                is_key = jnp.full(total.shape, kind, jnp.int32) == 0
                kv_ref[kind] = jnp.where(is_key, turned, total).astype(jnp.bfloat16)


def finish(core, parts, bias, cosine, sine):
    return pl.pallas_call(
        finish_kernel,
        out_shape=(
            jax.ShapeDtypeStruct((2, GROUP, PART, HD), jnp.bfloat16),
            jax.ShapeDtypeStruct((2, TOK, HD), jnp.bfloat16),
        ),
        in_specs=[pl.BlockSpec(memory_space=pltpu.SMEM)] + in_vmem(4),
        out_specs=tuple(in_vmem(2)),
        compiler_params=pltpu.CompilerParams(vmem_limit_bytes=VMEM),
    )(core, parts, bias, cosine, sine)


def with_ones(values):
    return jnp.concatenate([values, jnp.ones(values.shape, values.dtype)], axis=1)


def absorb(rows, query, keys, values, masks, peak_ref, acc_ref):
    scores = []
    for key, mask in zip(keys, masks, strict=True):
        score = lax.dot_general(
            query, key, (((1,), (1,)), ((), ())), preferred_element_type=jnp.float32
        )
        scores.append(score if mask is None else jnp.where(mask, score, LOWEST))
    old = peak_ref[rows, :]
    new = old
    for score in scores:
        new = jnp.maximum(new, jnp.max(score, axis=1, keepdims=True))
    fresh = None
    for score, value in zip(scores, values, strict=True):
        weights = jnp.exp2(score - new).astype(jnp.bfloat16)
        part = jnp.dot(weights, value, preferred_element_type=jnp.float32)
        fresh = part if fresh is None else fresh + part
    acc_ref[rows, :] = acc_ref[rows, :] * jnp.exp2(old - new) + fresh
    peak_ref[rows, :] = new


CHUNK = 256
ROWS = GROUP * TOK


def cache_kernel(distances, place_ref, q_ref, own_ref, peer_ref, acc_in, peak_in, acc_ref, peak_ref):
    offset = place_ref[0]
    core = place_ref[1]
    row = place_ref[2]
    if acc_in is None:
        acc_ref[...] = jnp.zeros_like(acc_ref)
        peak_ref[...] = jnp.full_like(peak_ref, LOWEST)
    else:
        acc_ref[...] = acc_in[...]
        peak_ref[...] = peak_in[...]

    def piece(index, carry):
        distance = distances[3]
        for at in range(3):
            distance = jnp.where(index == at, distances[at], distance)
        base = (row ^ distance) * SLOTS
        own_base = base + core * HALF
        peer_base = base + (1 - core) * HALF

        def step(masked):
            keys = [own_ref[index, 0], peer_ref[index, 0]]
            values = [with_ones(own_ref[index, 1]), with_ones(peer_ref[index, 1])]
            masks = [None, None]
            if masked:
                slot = lax.broadcasted_iota(jnp.int32, (CHUNK, HALF), 1)
                masks = [slot + own_base < offset, slot + peer_base < offset]
            for start in range(0, ROWS, CHUNK):
                rows = slice(start, start + CHUNK)
                absorb(rows, q_ref[rows, :], keys, values, masks, peak_ref, acc_ref)

        @pl.when(base + SLOTS <= offset)
        def _():
            step(False)

        @pl.when((base < offset) & (base + SLOTS > offset))
        def _():
            step(True)

        return carry

    lax.fori_loop(0, 4, piece, 0)


def first_cache_kernel(place_ref, q_ref, own_ref, peer_ref, acc_ref, peak_ref):
    cache_kernel(NEAR, place_ref, q_ref, own_ref, peer_ref, None, None, acc_ref, peak_ref)


def attend_cache(kernel, place, queries, own, peer, *state):
    return pl.pallas_call(
        kernel,
        out_shape=(
            jax.ShapeDtypeStruct((ROWS, 2 * HD), jnp.float32),
            jax.ShapeDtypeStruct((ROWS, 1), jnp.float32),
        ),
        in_specs=[pl.BlockSpec(memory_space=pltpu.SMEM)] + in_vmem(3 + len(state)),
        out_specs=tuple(in_vmem(2)),
        compiler_params=pltpu.CompilerParams(vmem_limit_bytes=VMEM),
        cost_estimate=pl.CostEstimate(
            flops=8 * 2**30, bytes_accessed=4 * 2**20, transcendentals=2**22
        ),
    )(place, queries, own, peer, *state)


def row_of(block, half):
    member, row = place_of(block)
    return MEMBERS[half][member], row


def span_kernel(
    place_ref, q_ref, own_ref, peer_ref, acc_in, peak_in, out_ref, acc_ref, peak_ref, k_ref, v_ref
):
    core = place_ref[1]
    half = place_ref[3]
    member = place_ref[4]
    acc_ref[...] = acc_in[...]
    peak_ref[...] = peak_in[...]
    v_ref[:, HD:] = jnp.ones((GROUP * 4 * PART, HD), jnp.bfloat16)
    for block in range(GROUP):
        for side, ref in enumerate((own_ref, peer_ref)):
            for part in range(2):
                device, row = row_of(block, part)
                start = block * 4 * PART + side * 2 * PART + part * PART
                k_ref[start : start + PART, :] = ref[device, 0, row : row + PART, :]
                v_ref[start : start + PART, :HD] = ref[device, 1, row : row + PART, :]
    width = GROUP * 2 * PART
    lane = lax.broadcasted_iota(jnp.int32, (CHUNK, width), 1)
    line = lax.broadcasted_iota(jnp.int32, (CHUNK, width), 0)
    within = lane % (2 * TOK)
    side_core = jnp.where(within < TOK, core, 1 - core)
    key_token = lane // (2 * TOK) * (2 * TOK) + side_core * TOK + within % TOK
    query_token = core * TOK + half * PART + line % PART
    for at in range(2):
        mine = member if at == 0 else 7 - member
        for begin in range(at * ROWS // 2, (at + 1) * ROWS // 2, CHUNK):
            rows = slice(begin, begin + CHUNK)
            keys, values, masks = [], [], []
            for first in range(0, (at + 1) * width, width):
                last = first == at * width
                keys.append(k_ref[first : first + width, :])
                values.append(v_ref[first : first + width, :])
                masks.append(
                    key_token + first <= query_token + mine * 2 * TOK if last else None
                )
            absorb(rows, q_ref[rows, :], keys, values, masks, peak_ref, acc_ref)
        for head in range(GROUP):
            first = at * ROWS // 2 + head * PART
            rows = slice(first, first + PART)
            out_ref[at * PART : (at + 1) * PART, head * HD : (head + 1) * HD] = (
                acc_ref[rows, :HD] / acc_ref[rows, HD:]
            ).astype(jnp.bfloat16)


def attend_span(place, queries, own, peer, acc, peak):
    return pl.pallas_call(
        span_kernel,
        out_shape=jax.ShapeDtypeStruct((TOK, GROUP * HD), jnp.bfloat16),
        in_specs=[pl.BlockSpec(memory_space=pltpu.SMEM)] + in_vmem(5),
        out_specs=pl.BlockSpec(memory_space=pltpu.VMEM),
        scratch_shapes=[
            pltpu.VMEM((ROWS, 2 * HD), jnp.float32),
            pltpu.VMEM((ROWS, 1), jnp.float32),
            pltpu.VMEM((GROUP * 4 * PART, HD), jnp.bfloat16),
            pltpu.VMEM((GROUP * 4 * PART, 2 * HD), jnp.bfloat16),
        ],
        compiler_params=pltpu.CompilerParams(vmem_limit_bytes=VMEM),
        cost_estimate=pl.CostEstimate(
            flops=3 * 2**30, bytes_accessed=4 * 2**20, transcendentals=2**21
        ),
    )(place, queries, own, peer, acc, peak)


def mix_kernel(a_ref, own_ref, peer_ref, own_x_ref, peer_x_ref, out_ref):
    a = a_ref[...].reshape(4 * TOK, GROUP * HD)
    width = 4 * HD
    for start, near, far in ((0, own_ref, peer_ref), (SLOTS, own_x_ref, peer_x_ref)):
        total = jnp.dot(a[:, :width], near[...], preferred_element_type=jnp.float32)
        total = total + jnp.dot(a[:, width:], far[...], preferred_element_type=jnp.float32)
        total = total.astype(jnp.bfloat16)
        for block in range(GROUP):
            member, row = place_of(block)
            row = row + member * TOK
            out_ref[block, :, start : start + SLOTS] = total[row : row + PART]


def mix(attended, *weights):
    return pl.pallas_call(
        mix_kernel,
        out_shape=jax.ShapeDtypeStruct((GROUP, PART, 2 * SLOTS), jnp.bfloat16),
        in_specs=in_vmem(5),
        out_specs=pl.BlockSpec(memory_space=pltpu.VMEM),
        compiler_params=pltpu.CompilerParams(vmem_limit_bytes=VMEM),
        cost_estimate=pl.CostEstimate(
            flops=2 * 2**30, bytes_accessed=7 * 2**20, transcendentals=0
        ),
    )(attended, *weights)


def body(
    hidden_in,
    norm_gain,
    w_query,
    scale_query,
    bias_query,
    w_keyval,
    scale_keyval,
    bias_keyval,
    w_out,
    scale_out,
    cache_keyval,
    span_offset,
):
    tie = lax.optimization_barrier
    row = lax.axis_index(ROW)
    x = lax.axis_index("x")
    head = lax.axis_index(COL)
    core = lax.axis_index("core")
    half = (x >> 1) ^ (x & 1)
    member = 2 * lax.axis_index("ylo") + (x >> 1)
    offset = span_offset[0]

    cached = lax.dynamic_slice(cache_keyval, (0, core * HALF, head * HD), (2, HALF, HD))
    cached_y = along(cached, "ylo", 2, 1)
    kept = lax.dynamic_slice_in_dim(hidden_in, half * PART, PART, 0)
    given = lax.dynamic_slice_in_dim(hidden_in, (1 - half) * PART, PART, 0)
    local = jnp.concatenate([kept, beside(given)], axis=1)
    local, cached_y = tie((local, cached_y))

    start = core * KVH + head
    weight = lax.dynamic_slice_in_dim(w_keyval, start * HD, HD, 1)
    scale = lax.dynamic_slice_in_dim(scale_keyval, start, 1, 1)
    weight = jnp.concatenate(
        [w_query.astype(jnp.float32) * expand(scale_query), weight.astype(jnp.float32) * expand(scale)],
        axis=1,
    )
    own = (weight * norm_gain[:, None]).astype(jnp.bfloat16)
    local, own = tie((local, own))
    gathered = exchange(copies(local, GROUP), COL)
    own_x = beside(own)
    peer = swap_cores(own)
    peer_x = swap_cores(own_x)

    bias = jnp.concatenate([bias_query, lax.dynamic_slice_in_dim(bias_keyval, start * HD, HD, 0)])
    bias = jnp.concatenate([bias, swap_cores(bias)])[None, :]

    pair = jnp.stack([cached, cached_y])
    near = jnp.concatenate([pair, along(pair, "x", 4, 3)], axis=0)
    near_peer = swap_cores(near)

    out_own = (w_out.astype(jnp.float32) * expand(scale_out)).astype(jnp.bfloat16)
    out_peer = swap_cores(out_own)

    index = jnp.arange(TOK, dtype=jnp.int32)
    block = jnp.where(index < PART, member, 7 - member)
    token = (2 * block + core) * TOK + half * PART + index % PART
    positions = (offset + token).astype(jnp.float32)
    inverse = ROPE_BASE ** (-(2.0 * jnp.arange(HD // 2, dtype=jnp.float32)) / HD)
    angles = positions[:, None] * inverse[None, :]
    cosine = jnp.cos(angles)
    sine = jnp.sin(angles)
    cosine = jnp.concatenate([cosine, cosine], axis=1)
    sine = jnp.concatenate([-sine, sine], axis=1)
    place = jnp.stack([offset, core, row, half, member]).astype(jnp.int32)

    near, own_x = tie((near, own_x))
    far = beside(near)
    gathered, bias, cosine, sine, place, out_own, out_peer, near_peer = tie(
        (gathered, bias, cosine, sine, place, out_own, out_peer, near_peer)
    )
    projected = project(gathered, own, own_x, peer, peer_x)
    parts = exchange(projected, ROW, MEMBERS)
    parts, out_own = tie((parts, out_own))
    out_own_x = beside(out_own)
    queries, own_kv = finish(place[1:2], parts, bias, cosine, sine)
    queries = queries.reshape(ROWS, HD)

    span_own = exchange(copies(own_kv, GROUP), ROW)
    state = attend_cache(first_cache_kernel, place, queries, near, near_peer)
    far_peer = swap_cores(far)
    span_own, state = tie((span_own, state))
    span_peer = swap_cores(span_own)
    state = attend_cache(
        functools.partial(cache_kernel, FAR), place, queries, far, far_peer, *state
    )
    attended = attend_span(place, queries, span_own, span_peer, *state)

    everyone = exchange(copies(attended, 4), ROW, MEMBERS)
    out_peer_x = swap_cores(out_own_x)
    mixed = mix(everyone, out_own, out_peer, out_own_x, out_peer_x)
    shares = exchange(mixed, COL)
    total = jnp.sum(shares.astype(jnp.float32), axis=0).astype(jnp.bfloat16)
    mine = total[:, :SLOTS]
    other = beside(total[:, SLOTS:])
    return jnp.where(
        half == 0, jnp.concatenate([mine, other]), jnp.concatenate([other, mine])
    )


def solution(mesh):
    fine = Mesh(mesh.devices.reshape(2, 4, 4, 2, 2), ("ylo", "x", "z", "yhi", "core"))
    row = ("ylo", "x")
    col = ("z", "yhi", "core")
    return jax.shard_map(
        body,
        mesh=fine,
        in_specs=(
            P(col, row),
            P(row),
            P(row, col),
            P(row, col),
            P(col),
            P(row, None),
            P(row, None),
            P(),
            P(col, row),
            P(col, row),
            P(None, row, None),
            P(),
        ),
        out_specs=P(col, row),
        check_vma=False,
    )
```

```python
import math

import jax
import jax.numpy as jnp
from jax import lax
from jax.experimental import pallas as pl
from jax.experimental.pallas import tpu as pltpu
from jax.sharding import Mesh
from jax.sharding import PartitionSpec as P

D = 8192
H = 64
KVH = 8
HD = 128
QB = 128
TOK = 128
GROUP = 8
SLOTS = 1024
HALF = 512

EPSILON = 1e-06
ROPE_BASE = 1000000.0
LOWEST = -1e30
ROW = ("ylo", "x")
COL = ("z", "yhi")
QSCALE = math.log2(math.e) / math.sqrt(HD)
WIDE = 640
SQUARES = 2 * WIDE
PART = 64
NEAR = (0, 4, 3, 7)
FAR = (1, 5, 2, 6)
MEMBERS = ((0, 3, 4, 7), (1, 2, 5, 6))
VMEM = 26 * 2**20


def expand(block_scale):
    return jnp.repeat(jnp.repeat(block_scale, QB, axis=0), QB, axis=1)


def swap_cores(array):
    return lax.ppermute(array, "core", [(0, 1), (1, 0)])


def along(array, axis, size, distance):
    return lax.ppermute(array, axis, [(i, i ^ distance) for i in range(size)])


def beside(array):
    return along(array, "x", 4, 1)


def exchange(array, axes, groups=None):
    return lax.all_to_all(array, axes, 0, 0, tiled=True, axis_index_groups=groups)


def copies(array, count):
    return jnp.broadcast_to(array[None], (count,) + array.shape)


def in_vmem(count):
    return [pl.BlockSpec(memory_space=pltpu.VMEM)] * count


def place_of(block):
    return (block, 0) if block < 4 else (7 - block, PART)


def project_kernel(x_ref, own_ref, own_x_ref, peer_ref, peer_x_ref, out_ref):
    rows = GROUP * PART
    x = x_ref[...].reshape(rows, 2 * SLOTS)
    for start, near, far in ((0, own_ref, own_x_ref), (WIDE, peer_ref, peer_x_ref)):
        total = jnp.dot(x[:, :SLOTS], near[...], preferred_element_type=jnp.float32)
        total = total + jnp.dot(x[:, SLOTS:], far[...], preferred_element_type=jnp.float32)
        total = total.astype(jnp.bfloat16)
        for block in range(GROUP):
            member, row = place_of(block)
            out_ref[member, row : row + PART, start : start + WIDE] = total[
                block * PART : (block + 1) * PART
            ]
    for block in range(GROUP):
        member, row = place_of(block)
        wide = x_ref[block].astype(jnp.float32)
        squares = jnp.sum(wide * wide, axis=1, keepdims=True)
        high = squares.astype(jnp.bfloat16).astype(jnp.float32)
        lane = lax.broadcasted_iota(jnp.int32, (PART, HD), 1)
        both = jnp.where(lane < HD // 2, high, squares - high)
        out_ref[member, row : row + PART, SQUARES:] = both.astype(jnp.bfloat16)


def project(x, *weights):
    return pl.pallas_call(
        project_kernel,
        out_shape=jax.ShapeDtypeStruct((4, TOK, SQUARES + HD), jnp.bfloat16),
        in_specs=in_vmem(5),
        out_specs=pl.BlockSpec(memory_space=pltpu.VMEM),
        compiler_params=pltpu.CompilerParams(vmem_limit_bytes=VMEM),
        cost_estimate=pl.CostEstimate(
            flops=3 * 2**30, bytes_accessed=9 * 2**20, transcendentals=0
        ),
    )(x, *weights)


def finish_kernel(core_ref, parts_ref, bias_ref, turns_ref, q_ref, kv_ref):
    core = core_ref[0]
    turns = turns_ref[...]
    turned_turns = pltpu.roll(turns, HD // 2, 1)
    low = lax.broadcasted_iota(jnp.int32, turns.shape, 1) < HD // 2
    cosine = jnp.where(low, turns, turned_turns)
    sine = jnp.where(low, -turned_turns, turns)

    def summed(start):
        total = parts_ref[0, :, start : start + HD].astype(jnp.float32)
        for part in range(1, 4):
            total = total + parts_ref[part, :, start : start + HD].astype(jnp.float32)
        return total

    squares = summed(SQUARES)
    ratio = lax.rsqrt((squares[:, :1] + squares[:, HD // 2 : HD // 2 + 1]) / D + EPSILON)
    for side in range(2):
        for column in range(5):
            start = side * WIDE + column * HD
            total = summed(start) * ratio + bias_ref[:, start : start + HD]
            turned = total * cosine + pltpu.roll(total, HD // 2, 1) * sine
            if column < 4:
                turned = (turned * QSCALE).astype(jnp.bfloat16)
                q_ref[0, side * 4 + column] = turned[:PART]
                q_ref[1, side * 4 + column] = turned[PART:]
            else:
                kind = core if side == 0 else 1 - core
                is_key = jnp.full(total.shape, kind, jnp.int32) == 0
                kv_ref[kind] = jnp.where(is_key, turned, total).astype(jnp.bfloat16)


def finish(core, parts, bias, turns):
    return pl.pallas_call(
        finish_kernel,
        out_shape=(
            jax.ShapeDtypeStruct((2, GROUP, PART, HD), jnp.bfloat16),
            jax.ShapeDtypeStruct((2, TOK, HD), jnp.bfloat16),
        ),
        in_specs=[pl.BlockSpec(memory_space=pltpu.SMEM)] + in_vmem(3),
        out_specs=tuple(in_vmem(2)),
        compiler_params=pltpu.CompilerParams(vmem_limit_bytes=VMEM),
    )(core, parts, bias, turns)


def with_ones(values):
    return jnp.concatenate([values, jnp.ones(values.shape, values.dtype)], axis=1)


def absorb(rows, query, keys, values, masks, peak_ref, acc_ref):
    scores = []
    for key, mask in zip(keys, masks, strict=True):
        score = lax.dot_general(
            query, key, (((1,), (1,)), ((), ())), preferred_element_type=jnp.float32
        )
        scores.append(score if mask is None else jnp.where(mask, score, LOWEST))
    old = peak_ref[rows, :]
    new = old
    for score in scores:
        new = jnp.maximum(new, jnp.max(score, axis=1, keepdims=True))
    fresh = None
    for score, value in zip(scores, values, strict=True):
        weights = jnp.exp2(score - new).astype(jnp.bfloat16)
        part = jnp.dot(weights, value, preferred_element_type=jnp.float32)
        fresh = part if fresh is None else fresh + part
    acc_ref[rows, :] = acc_ref[rows, :] * jnp.exp2(old - new) + fresh
    peak_ref[rows, :] = new


CHUNK = 128
ROWS = GROUP * TOK


def cache_kernel(
    place_ref,
    q_ref,
    near_own,
    near_peer,
    far_own,
    far_peer,
    acc_ref,
    peak_ref,
    own_ref,
    peer_ref,
    sems,
):
    offset = place_ref[0]
    core = place_ref[1]
    row = place_ref[2]
    groups = ((NEAR, near_own, near_peer), (FAR, far_own, far_peer))

    def fetch(group, index):
        own_hbm, peer_hbm = groups[group][1:]
        at = group * 4 + index
        return (
            pltpu.make_async_copy(own_hbm.at[index], own_ref.at[at], sems.at[0, at]),
            pltpu.make_async_copy(peer_hbm.at[index], peer_ref.at[at], sems.at[1, at]),
        )

    for group in range(2):
        for index in range(4):
            for copy in fetch(group, index):
                copy.start()
    acc_ref[...] = jnp.zeros_like(acc_ref)
    peak_ref[...] = jnp.full_like(peak_ref, LOWEST)

    def piece(group, index):
        distances = groups[group][0]
        distance = distances[3]
        for at in range(3):
            distance = jnp.where(index == at, distances[at], distance)
        for copy in fetch(group, index):
            copy.wait()
        held = group * 4 + index
        base = (row ^ distance) * SLOTS
        own_base = base + core * HALF
        peer_base = base + (1 - core) * HALF

        def step(masked):
            keys = [own_ref[held, 0], peer_ref[held, 0]]
            values = [with_ones(own_ref[held, 1]), with_ones(peer_ref[held, 1])]
            masks = [None, None]
            if masked:
                slot = lax.broadcasted_iota(jnp.int32, (CHUNK, HALF), 1)
                masks = [slot + own_base < offset, slot + peer_base < offset]
            for start in range(0, ROWS, CHUNK):
                rows = slice(start, start + CHUNK)
                absorb(rows, q_ref[rows, :], keys, values, masks, peak_ref, acc_ref)

        @pl.when(base + SLOTS <= offset)
        def _():
            step(False)

        @pl.when((base < offset) & (base + SLOTS > offset))
        def _():
            step(True)

    for group in range(2):

        def one(index, carry, group=group):
            piece(group, index)
            return carry

        lax.fori_loop(0, 4, one, 0)


def attend_cache(place, queries, *pieces):
    return pl.pallas_call(
        cache_kernel,
        out_shape=(
            jax.ShapeDtypeStruct((ROWS, 2 * HD), jnp.float32),
            jax.ShapeDtypeStruct((ROWS, 1), jnp.float32),
        ),
        in_specs=[pl.BlockSpec(memory_space=pltpu.SMEM)]
        + in_vmem(1)
        + [pl.BlockSpec(memory_space=pl.ANY)] * 4,
        out_specs=tuple(in_vmem(2)),
        scratch_shapes=[
            pltpu.VMEM((8, 2, HALF, HD), jnp.bfloat16),
            pltpu.VMEM((8, 2, HALF, HD), jnp.bfloat16),
            pltpu.SemaphoreType.DMA((2, 8)),
        ],
        compiler_params=pltpu.CompilerParams(vmem_limit_bytes=VMEM),
        cost_estimate=pl.CostEstimate(
            flops=16 * 2**30, bytes_accessed=8 * 2**20, transcendentals=2**23
        ),
    )(place, queries, *pieces)


def row_of(block, half):
    member, row = place_of(block)
    return MEMBERS[half][member], row


def span_kernel(
    place_ref, q_ref, span_ref, acc_in, peak_in, out_ref, acc_ref, peak_ref, k_ref, v_ref
):
    core = place_ref[1]
    half = place_ref[3]
    member = place_ref[4]
    acc_ref[...] = acc_in[...]
    peak_ref[...] = peak_in[...]
    v_ref[:, HD:] = jnp.ones((GROUP * 4 * PART, HD), jnp.bfloat16)
    for block in range(GROUP):
        for side in range(2):
            for part in range(2):
                device, row = row_of(block, part)
                start = block * 4 * PART + side * 2 * PART + part * PART
                k_ref[start : start + PART, :] = span_ref[device, side, 0, row : row + PART, :]
                v_ref[start : start + PART, :HD] = span_ref[device, side, 1, row : row + PART, :]
    width = GROUP * 2 * PART
    lane = lax.broadcasted_iota(jnp.int32, (CHUNK, width), 1)
    line = lax.broadcasted_iota(jnp.int32, (CHUNK, width), 0)
    within = lane % (2 * TOK)
    side_core = jnp.where(within < TOK, core, 1 - core)
    key_token = lane // (2 * TOK) * (2 * TOK) + side_core * TOK + within % TOK
    query_token = core * TOK + half * PART + line % PART
    for at in range(2):
        mine = member if at == 0 else 7 - member
        for begin in range(at * ROWS // 2, (at + 1) * ROWS // 2, CHUNK):
            rows = slice(begin, begin + CHUNK)
            keys, values, masks = [], [], []
            for first in range(0, (at + 1) * width, width):
                last = first == at * width
                keys.append(k_ref[first : first + width, :])
                values.append(v_ref[first : first + width, :])
                masks.append(
                    key_token + first <= query_token + mine * 2 * TOK if last else None
                )
            absorb(rows, q_ref[rows, :], keys, values, masks, peak_ref, acc_ref)
        for head in range(GROUP):
            first = at * ROWS // 2 + head * PART
            rows = slice(first, first + PART)
            out_ref[at * PART : (at + 1) * PART, head * HD : (head + 1) * HD] = (
                acc_ref[rows, :HD] / acc_ref[rows, HD:]
            ).astype(jnp.bfloat16)


def attend_span(place, queries, span, acc, peak):
    return pl.pallas_call(
        span_kernel,
        out_shape=jax.ShapeDtypeStruct((TOK, GROUP * HD), jnp.bfloat16),
        in_specs=[pl.BlockSpec(memory_space=pltpu.SMEM)] + in_vmem(4),
        out_specs=pl.BlockSpec(memory_space=pltpu.VMEM),
        scratch_shapes=[
            pltpu.VMEM((ROWS, 2 * HD), jnp.float32),
            pltpu.VMEM((ROWS, 1), jnp.float32),
            pltpu.VMEM((GROUP * 4 * PART, HD), jnp.bfloat16),
            pltpu.VMEM((GROUP * 4 * PART, 2 * HD), jnp.bfloat16),
        ],
        compiler_params=pltpu.CompilerParams(vmem_limit_bytes=VMEM),
        cost_estimate=pl.CostEstimate(
            flops=3 * 2**30, bytes_accessed=4 * 2**20, transcendentals=2**21
        ),
    )(place, queries, span, acc, peak)


def mix_kernel(a_ref, own_ref, peer_ref, own_x_ref, peer_x_ref, out_ref):
    a = a_ref[...].reshape(4 * TOK, GROUP * HD)
    width = 4 * HD
    for start, near, far in ((0, own_ref, peer_ref), (SLOTS, own_x_ref, peer_x_ref)):
        total = jnp.dot(a[:, :width], near[...], preferred_element_type=jnp.float32)
        total = total + jnp.dot(a[:, width:], far[...], preferred_element_type=jnp.float32)
        total = total.astype(jnp.bfloat16)
        for block in range(GROUP):
            member, row = place_of(block)
            row = row + member * TOK
            out_ref[block, :, start : start + SLOTS] = total[row : row + PART]


def mix(attended, *weights):
    return pl.pallas_call(
        mix_kernel,
        out_shape=jax.ShapeDtypeStruct((GROUP, PART, 2 * SLOTS), jnp.bfloat16),
        in_specs=in_vmem(5),
        out_specs=pl.BlockSpec(memory_space=pltpu.VMEM),
        compiler_params=pltpu.CompilerParams(vmem_limit_bytes=VMEM),
        cost_estimate=pl.CostEstimate(
            flops=2 * 2**30, bytes_accessed=7 * 2**20, transcendentals=0
        ),
    )(attended, *weights)


def body(
    hidden_in,
    norm_gain,
    w_query,
    scale_query,
    bias_query,
    w_keyval,
    scale_keyval,
    bias_keyval,
    w_out,
    scale_out,
    cache_keyval,
    span_offset,
):
    tie = lax.optimization_barrier
    row = lax.axis_index(ROW)
    x = lax.axis_index("x")
    head = lax.axis_index(COL)
    core = lax.axis_index("core")
    half = (x >> 1) ^ (x & 1)
    member = 2 * lax.axis_index("ylo") + (x >> 1)
    offset = span_offset[0]

    cached = lax.dynamic_slice(cache_keyval, (0, core * HALF, head * HD), (2, HALF, HD))
    cached_y = along(cached, "ylo", 2, 1)
    kept = lax.dynamic_slice_in_dim(hidden_in, half * PART, PART, 0)
    given = lax.dynamic_slice_in_dim(hidden_in, (1 - half) * PART, PART, 0)
    local = jnp.concatenate([kept, beside(given)], axis=1)
    local, cached_y = tie((local, cached_y))
    gathered = exchange(copies(local, GROUP), COL)

    start = core * KVH + head
    weight = lax.dynamic_slice_in_dim(w_keyval, start * HD, HD, 1)
    scale = lax.dynamic_slice_in_dim(scale_keyval, start, 1, 1)
    weight = jnp.concatenate(
        [w_query.astype(jnp.float32) * expand(scale_query), weight.astype(jnp.float32) * expand(scale)],
        axis=1,
    )
    own = (weight * norm_gain[:, None]).astype(jnp.bfloat16)
    local, own = tie((local, own))
    own_x = beside(own)
    peer = swap_cores(own)
    peer_x = swap_cores(own_x)

    bias = jnp.concatenate([bias_query, lax.dynamic_slice_in_dim(bias_keyval, start * HD, HD, 0)])
    bias = jnp.concatenate([bias, swap_cores(bias)])[None, :]

    pair = jnp.stack([cached, cached_y])
    near = jnp.concatenate([pair, along(pair, "x", 4, 3)], axis=0)
    near_peer = swap_cores(near)

    out_own = (w_out.astype(jnp.float32) * expand(scale_out)).astype(jnp.bfloat16)
    out_peer = swap_cores(out_own)

    index = jnp.arange(TOK, dtype=jnp.int32)
    block = jnp.where(index < PART, member, 7 - member)
    token = (2 * block + core) * TOK + half * PART + index % PART
    positions = (offset + token).astype(jnp.float32)
    inverse = ROPE_BASE ** (-(2.0 * jnp.arange(HD // 2, dtype=jnp.float32)) / HD)
    angles = positions[:, None] * inverse[None, :]
    turns = jnp.concatenate([jnp.cos(angles), jnp.sin(angles)], axis=1)
    place = jnp.stack([offset, core, row, half, member]).astype(jnp.int32)

    near, own_x = tie((near, own_x))
    far = beside(near)
    gathered, bias, turns, place, out_own, out_peer, near_peer = tie(
        (gathered, bias, turns, place, out_own, out_peer, near_peer)
    )
    projected = project(gathered, own, own_x, peer, peer_x)
    parts = exchange(projected, ROW, MEMBERS)
    queries, own_kv = finish(place[1:2], parts, bias, turns)
    queries = queries.reshape(ROWS, HD)

    pair_kv = jnp.stack([own_kv, swap_cores(own_kv)])
    queries, pair_kv = tie((queries, copies(pair_kv, GROUP)))
    span = exchange(pair_kv, ROW)
    state = attend_cache(place, queries, near, near_peer, far, swap_cores(far))
    state, span, out_own = tie((state, span, out_own))
    out_own_x = beside(out_own)
    attended = attend_span(place, queries, span, *state)

    everyone = exchange(copies(attended, 4), ROW, MEMBERS)
    everyone, out_own_x = tie((everyone, out_own_x))
    out_peer_x = swap_cores(out_own_x)
    mixed = mix(everyone, out_own, out_peer, out_own_x, out_peer_x)
    shares = exchange(mixed, COL)
    total = jnp.sum(shares.astype(jnp.float32), axis=0).astype(jnp.bfloat16)
    mine = total[:, :SLOTS]
    other = beside(total[:, SLOTS:])
    return jnp.where(
        half == 0, jnp.concatenate([mine, other]), jnp.concatenate([other, mine])
    )


def solution(mesh):
    fine = Mesh(mesh.devices.reshape(2, 4, 4, 2, 2), ("ylo", "x", "z", "yhi", "core"))
    row = ("ylo", "x")
    col = ("z", "yhi", "core")
    return jax.shard_map(
        body,
        mesh=fine,
        in_specs=(
            P(col, row),
            P(row),
            P(row, col),
            P(row, col),
            P(col),
            P(row, None),
            P(row, None),
            P(),
            P(col, row),
            P(col, row),
            P(None, row, None),
            P(),
        ),
        out_specs=P(col, row),
        check_vma=False,
    )
```

```python
import math

import jax
import jax.numpy as jnp
from jax import lax
from jax.experimental import pallas as pl
from jax.experimental.pallas import tpu as pltpu
from jax.sharding import Mesh
from jax.sharding import PartitionSpec as P

D = 8192
H = 64
KVH = 8
HD = 128
QB = 128
TOK = 128
GROUP = 8
SLOTS = 1024
HALF = 512

EPSILON = 1e-06
ROPE_BASE = 1000000.0
LOWEST = -1e30
ROW = ("ylo", "x")
COL = ("z", "yhi")
QSCALE = math.log2(math.e) / math.sqrt(HD)
WIDE = 640
SQUARES = 2 * WIDE
PART = 64
NEAR = (0, 4, 3, 7)
FAR = (1, 5, 2, 6)
MEMBERS = ((0, 3, 4, 7), (1, 2, 5, 6))
PAIRS = (tuple(range(16)), tuple(range(16, 32)))
VMEM = 26 * 2**20


def expand(block_scale):
    return jnp.repeat(jnp.repeat(block_scale, QB, axis=0), QB, axis=1)


def swap_cores(array):
    return lax.ppermute(array, "core", [(0, 1), (1, 0)])


def along(array, axis, size, distance):
    return lax.ppermute(array, axis, [(i, i ^ distance) for i in range(size)])


def beside(array):
    return along(array, "x", 4, 1)


def exchange(array, axes, groups=None):
    return lax.all_to_all(array, axes, 0, 0, tiled=True, axis_index_groups=groups)


def copies(array, count):
    return jnp.broadcast_to(array[None], (count,) + array.shape)


def in_vmem(count):
    return [pl.BlockSpec(memory_space=pltpu.VMEM)] * count


def place_of(block):
    return (block, 0) if block < 4 else (7 - block, PART)


def project_kernel(x_ref, own_ref, own_x_ref, peer_ref, peer_x_ref, out_ref):
    rows = GROUP * PART
    x = x_ref[...].reshape(rows, 2 * SLOTS)
    for start, near, far in ((0, own_ref, own_x_ref), (WIDE, peer_ref, peer_x_ref)):
        total = jnp.dot(x[:, :SLOTS], near[...], preferred_element_type=jnp.float32)
        total = total + jnp.dot(x[:, SLOTS:], far[...], preferred_element_type=jnp.float32)
        total = total.astype(jnp.bfloat16)
        for block in range(GROUP):
            member, row = place_of(block)
            out_ref[member, row : row + PART, start : start + WIDE] = total[
                block * PART : (block + 1) * PART
            ]
    for block in range(GROUP):
        member, row = place_of(block)
        wide = x_ref[block].astype(jnp.float32)
        squares = jnp.sum(wide * wide, axis=1, keepdims=True)
        high = squares.astype(jnp.bfloat16).astype(jnp.float32)
        lane = lax.broadcasted_iota(jnp.int32, (PART, HD), 1)
        both = jnp.where(lane < HD // 2, high, squares - high)
        out_ref[member, row : row + PART, SQUARES:] = both.astype(jnp.bfloat16)


def project(x, *weights):
    return pl.pallas_call(
        project_kernel,
        out_shape=jax.ShapeDtypeStruct((4, TOK, SQUARES + HD), jnp.bfloat16),
        in_specs=in_vmem(5),
        out_specs=pl.BlockSpec(memory_space=pltpu.VMEM),
        compiler_params=pltpu.CompilerParams(vmem_limit_bytes=VMEM),
        cost_estimate=pl.CostEstimate(
            flops=3 * 2**30, bytes_accessed=9 * 2**20, transcendentals=0
        ),
    )(x, *weights)


def finish_kernel(core_ref, parts_ref, bias_ref, turns_ref, q_ref, kv_ref):
    core = core_ref[0]
    turns = turns_ref[...]
    turned_turns = pltpu.roll(turns, HD // 2, 1)
    low = lax.broadcasted_iota(jnp.int32, turns.shape, 1) < HD // 2
    cosine = jnp.where(low, turns, turned_turns)
    sine = jnp.where(low, -turned_turns, turns)

    def summed(start):
        total = parts_ref[0, :, start : start + HD].astype(jnp.float32)
        for part in range(1, 4):
            total = total + parts_ref[part, :, start : start + HD].astype(jnp.float32)
        return total

    squares = summed(SQUARES)
    ratio = lax.rsqrt((squares[:, :1] + squares[:, HD // 2 : HD // 2 + 1]) / D + EPSILON)
    for side in range(2):
        for column in range(5):
            start = side * WIDE + column * HD
            total = summed(start) * ratio + bias_ref[:, start : start + HD]
            turned = total * cosine + pltpu.roll(total, HD // 2, 1) * sine
            if column < 4:
                turned = (turned * QSCALE).astype(jnp.bfloat16)
                q_ref[0, side * 4 + column] = turned[:PART]
                q_ref[1, side * 4 + column] = turned[PART:]
            else:
                kind = core if side == 0 else 1 - core
                is_key = jnp.full(total.shape, kind, jnp.int32) == 0
                kv_ref[kind] = jnp.where(is_key, turned, total).astype(jnp.bfloat16)


def finish(core, parts, bias, turns):
    return pl.pallas_call(
        finish_kernel,
        out_shape=(
            jax.ShapeDtypeStruct((2, GROUP, PART, HD), jnp.bfloat16),
            jax.ShapeDtypeStruct((2, TOK, HD), jnp.bfloat16),
        ),
        in_specs=[pl.BlockSpec(memory_space=pltpu.SMEM)] + in_vmem(3),
        out_specs=tuple(in_vmem(2)),
        compiler_params=pltpu.CompilerParams(vmem_limit_bytes=VMEM),
    )(core, parts, bias, turns)


def with_ones(values):
    return jnp.concatenate([values, jnp.ones(values.shape, values.dtype)], axis=1)


def absorb(rows, query, keys, values, masks, peak_ref, acc_ref):
    scores = []
    for key, mask in zip(keys, masks, strict=True):
        score = lax.dot_general(
            query, key, (((1,), (1,)), ((), ())), preferred_element_type=jnp.float32
        )
        scores.append(score if mask is None else jnp.where(mask, score, LOWEST))
    old = peak_ref[rows, :]
    new = old
    for score in scores:
        new = jnp.maximum(new, jnp.max(score, axis=1, keepdims=True))
    fresh = None
    for score, value in zip(scores, values, strict=True):
        weights = jnp.exp2(score - new).astype(jnp.bfloat16)
        part = jnp.dot(weights, value, preferred_element_type=jnp.float32)
        fresh = part if fresh is None else fresh + part
    acc_ref[rows, :] = acc_ref[rows, :] * jnp.exp2(old - new) + fresh
    peak_ref[rows, :] = new


CHUNK = 128
ROWS = GROUP * TOK


def cache_kernel(
    place_ref,
    q_ref,
    near_own,
    near_peer,
    far_own,
    far_peer,
    acc_ref,
    peak_ref,
    own_ref,
    peer_ref,
    sems,
):
    offset = place_ref[0]
    core = place_ref[1]
    row = place_ref[2]
    groups = ((NEAR, near_own, near_peer), (FAR, far_own, far_peer))

    def fetch(group, index):
        own_hbm, peer_hbm = groups[group][1:]
        at = group * 4 + index
        return (
            pltpu.make_async_copy(own_hbm.at[index], own_ref.at[at], sems.at[0, at]),
            pltpu.make_async_copy(peer_hbm.at[index], peer_ref.at[at], sems.at[1, at]),
        )

    for group in range(2):
        for index in range(4):
            for copy in fetch(group, index):
                copy.start()
    acc_ref[...] = jnp.zeros_like(acc_ref)
    peak_ref[...] = jnp.full_like(peak_ref, LOWEST)

    def piece(group, index):
        distances = groups[group][0]
        distance = distances[3]
        for at in range(3):
            distance = jnp.where(index == at, distances[at], distance)
        for copy in fetch(group, index):
            copy.wait()
        held = group * 4 + index
        base = (row ^ distance) * SLOTS
        own_base = base + core * HALF
        peer_base = base + (1 - core) * HALF

        def step(masked):
            keys = [own_ref[held, 0], peer_ref[held, 0]]
            values = [with_ones(own_ref[held, 1]), with_ones(peer_ref[held, 1])]
            masks = [None, None]
            if masked:
                slot = lax.broadcasted_iota(jnp.int32, (CHUNK, HALF), 1)
                masks = [slot + own_base < offset, slot + peer_base < offset]
            for start in range(0, ROWS, CHUNK):
                rows = slice(start, start + CHUNK)
                absorb(rows, q_ref[rows, :], keys, values, masks, peak_ref, acc_ref)

        @pl.when(base + SLOTS <= offset)
        def _():
            step(False)

        @pl.when((base < offset) & (base + SLOTS > offset))
        def _():
            step(True)

    for group in range(2):

        def one(index, carry, group=group):
            piece(group, index)
            return carry

        lax.fori_loop(0, 4, one, 0)


def attend_cache(place, queries, *pieces):
    return pl.pallas_call(
        cache_kernel,
        out_shape=(
            jax.ShapeDtypeStruct((ROWS, 2 * HD), jnp.float32),
            jax.ShapeDtypeStruct((ROWS, 1), jnp.float32),
        ),
        in_specs=[pl.BlockSpec(memory_space=pltpu.SMEM)]
        + in_vmem(1)
        + [pl.BlockSpec(memory_space=pl.ANY)] * 4,
        out_specs=tuple(in_vmem(2)),
        scratch_shapes=[
            pltpu.VMEM((8, 2, HALF, HD), jnp.bfloat16),
            pltpu.VMEM((8, 2, HALF, HD), jnp.bfloat16),
            pltpu.SemaphoreType.DMA((2, 8)),
        ],
        compiler_params=pltpu.CompilerParams(vmem_limit_bytes=VMEM),
        cost_estimate=pl.CostEstimate(
            flops=16 * 2**30, bytes_accessed=8 * 2**20, transcendentals=2**23
        ),
    )(place, queries, *pieces)


def row_of(block, half):
    member, row = place_of(block)
    return MEMBERS[half][member], row


def span_kernel(
    place_ref, q_ref, span_ref, acc_in, peak_in, out_ref, acc_ref, peak_ref, k_ref, v_ref
):
    core = place_ref[1]
    half = place_ref[3]
    member = place_ref[4]
    acc_ref[...] = acc_in[...]
    peak_ref[...] = peak_in[...]
    v_ref[:, HD:] = jnp.ones((GROUP * 4 * PART, HD), jnp.bfloat16)
    for block in range(GROUP):
        for side in range(2):
            for part in range(2):
                device, row = row_of(block, part)
                start = block * 4 * PART + side * 2 * PART + part * PART
                k_ref[start : start + PART, :] = span_ref[device, side, 0, row : row + PART, :]
                v_ref[start : start + PART, :HD] = span_ref[device, side, 1, row : row + PART, :]
    width = GROUP * 2 * PART
    lane = lax.broadcasted_iota(jnp.int32, (CHUNK, width), 1)
    line = lax.broadcasted_iota(jnp.int32, (CHUNK, width), 0)
    within = lane % (2 * TOK)
    side_core = jnp.where(within < TOK, core, 1 - core)
    key_token = lane // (2 * TOK) * (2 * TOK) + side_core * TOK + within % TOK
    query_token = core * TOK + half * PART + line % PART
    for at in range(2):
        mine = member if at == 0 else 7 - member
        for begin in range(at * ROWS // 2, (at + 1) * ROWS // 2, CHUNK):
            rows = slice(begin, begin + CHUNK)
            keys, values, masks = [], [], []
            for first in range(0, (at + 1) * width, width):
                last = first == at * width
                keys.append(k_ref[first : first + width, :])
                values.append(v_ref[first : first + width, :])
                masks.append(
                    key_token + first <= query_token + mine * 2 * TOK if last else None
                )
            absorb(rows, q_ref[rows, :], keys, values, masks, peak_ref, acc_ref)
        for head in range(GROUP):
            first = at * ROWS // 2 + head * PART
            rows = slice(first, first + PART)
            out_ref[at * PART : (at + 1) * PART, head * HD : (head + 1) * HD] = (
                acc_ref[rows, :HD] / acc_ref[rows, HD:]
            ).astype(jnp.bfloat16)


def attend_span(place, queries, span, acc, peak):
    return pl.pallas_call(
        span_kernel,
        out_shape=jax.ShapeDtypeStruct((TOK, GROUP * HD), jnp.bfloat16),
        in_specs=[pl.BlockSpec(memory_space=pltpu.SMEM)] + in_vmem(4),
        out_specs=pl.BlockSpec(memory_space=pltpu.VMEM),
        scratch_shapes=[
            pltpu.VMEM((ROWS, 2 * HD), jnp.float32),
            pltpu.VMEM((ROWS, 1), jnp.float32),
            pltpu.VMEM((GROUP * 4 * PART, HD), jnp.bfloat16),
            pltpu.VMEM((GROUP * 4 * PART, 2 * HD), jnp.bfloat16),
        ],
        compiler_params=pltpu.CompilerParams(vmem_limit_bytes=VMEM),
        cost_estimate=pl.CostEstimate(
            flops=3 * 2**30, bytes_accessed=4 * 2**20, transcendentals=2**21
        ),
    )(place, queries, span, acc, peak)


def mix_kernel(side_ref, a_ref, own_ref, peer_ref, own_x_ref, peer_x_ref, out_ref):
    a = a_ref[...].reshape(4 * TOK, GROUP * HD)
    width = 4 * HD

    def fill(side):
        for to, near, far in ((side, own_ref, peer_ref), (1 - side, own_x_ref, peer_x_ref)):
            total = jnp.dot(a[:, :width], near[...], preferred_element_type=jnp.float32)
            total = total + jnp.dot(a[:, width:], far[...], preferred_element_type=jnp.float32)
            total = total.astype(jnp.bfloat16)
            for block in range(GROUP):
                member, row = place_of(block)
                row = row + member * TOK
                out_ref[to, block] = total[row : row + PART]

    for side in range(2):

        @pl.when(side_ref[0] == side)
        def _(side=side):
            fill(side)


def mix(side, attended, *weights):
    return pl.pallas_call(
        mix_kernel,
        out_shape=jax.ShapeDtypeStruct((2, GROUP, PART, SLOTS), jnp.bfloat16),
        in_specs=[pl.BlockSpec(memory_space=pltpu.SMEM)] + in_vmem(5),
        out_specs=pl.BlockSpec(memory_space=pltpu.VMEM),
        compiler_params=pltpu.CompilerParams(vmem_limit_bytes=VMEM),
        cost_estimate=pl.CostEstimate(
            flops=2 * 2**30, bytes_accessed=7 * 2**20, transcendentals=0
        ),
    )(side, attended, *weights)


def body(
    hidden_in,
    norm_gain,
    w_query,
    scale_query,
    bias_query,
    w_keyval,
    scale_keyval,
    bias_keyval,
    w_out,
    scale_out,
    cache_keyval,
    span_offset,
):
    tie = lax.optimization_barrier
    row = lax.axis_index(ROW)
    x = lax.axis_index("x")
    head = lax.axis_index(COL)
    core = lax.axis_index("core")
    half = (x >> 1) ^ (x & 1)
    member = 2 * lax.axis_index("ylo") + (x >> 1)
    offset = span_offset[0]

    cached = lax.dynamic_slice(cache_keyval, (0, core * HALF, head * HD), (2, HALF, HD))
    cached_y = along(cached, "ylo", 2, 1)
    kept = lax.dynamic_slice_in_dim(hidden_in, half * PART, PART, 0)
    given = lax.dynamic_slice_in_dim(hidden_in, (1 - half) * PART, PART, 0)
    local = jnp.concatenate([kept, beside(given)], axis=1)
    local, cached_y = tie((local, cached_y))
    gathered = exchange(copies(local, GROUP), COL)

    start = core * KVH + head
    weight = lax.dynamic_slice_in_dim(w_keyval, start * HD, HD, 1)
    scale = lax.dynamic_slice_in_dim(scale_keyval, start, 1, 1)
    weight = jnp.concatenate(
        [w_query.astype(jnp.float32) * expand(scale_query), weight.astype(jnp.float32) * expand(scale)],
        axis=1,
    )
    own = (weight * norm_gain[:, None]).astype(jnp.bfloat16)
    local, own = tie((local, own))
    own_x = beside(own)
    peer = swap_cores(own)
    peer_x = swap_cores(own_x)

    bias = jnp.concatenate([bias_query, lax.dynamic_slice_in_dim(bias_keyval, start * HD, HD, 0)])
    bias = jnp.concatenate([bias, swap_cores(bias)])[None, :]

    pair = jnp.stack([cached, cached_y])
    near = jnp.concatenate([pair, along(pair, "x", 4, 3)], axis=0)
    near_peer = swap_cores(near)

    out_own = (w_out.astype(jnp.float32) * expand(scale_out)).astype(jnp.bfloat16)
    out_peer = swap_cores(out_own)

    index = jnp.arange(TOK, dtype=jnp.int32)
    block = jnp.where(index < PART, member, 7 - member)
    token = (2 * block + core) * TOK + half * PART + index % PART
    positions = (offset + token).astype(jnp.float32)
    inverse = ROPE_BASE ** (-(2.0 * jnp.arange(HD // 2, dtype=jnp.float32)) / HD)
    angles = positions[:, None] * inverse[None, :]
    turns = jnp.concatenate([jnp.cos(angles), jnp.sin(angles)], axis=1)
    place = jnp.stack([offset, core, row, half, member]).astype(jnp.int32)

    near, own_x = tie((near, own_x))
    far = beside(near)
    gathered, bias, turns, place, out_own, out_peer, near_peer = tie(
        (gathered, bias, turns, place, out_own, out_peer, near_peer)
    )
    projected = project(gathered, own, own_x, peer, peer_x)
    parts = exchange(projected, ROW, MEMBERS)
    queries, own_kv = finish(place[1:2], parts, bias, turns)
    queries = queries.reshape(ROWS, HD)

    pair_kv = jnp.stack([own_kv, swap_cores(own_kv)])
    queries, pair_kv = tie((queries, copies(pair_kv, GROUP)))
    span = exchange(pair_kv, ROW)
    state = attend_cache(place, queries, near, near_peer, far, swap_cores(far))
    state, out_own = tie((state, out_own))
    out_own_x = beside(out_own)
    attended = attend_span(place, queries, span, *state)

    everyone = exchange(copies(attended, 4), ROW, MEMBERS)
    everyone, out_own_x = tie((everyone, out_own_x))
    out_peer_x = swap_cores(out_own_x)
    side = jnp.reshape(x & 1, (1,)).astype(jnp.int32)
    mixed = mix(side, everyone, out_own, out_peer, out_own_x, out_peer_x)
    shares = exchange(mixed.reshape(2 * GROUP, PART, SLOTS), ("x",) + COL, PAIRS)
    shares = shares.reshape(2, GROUP, PART, SLOTS).astype(jnp.float32)
    total = jnp.sum(shares, axis=1).astype(jnp.bfloat16)
    return jnp.where(x < 2, total, total[::-1]).reshape(TOK, SLOTS)


def solution(mesh):
    fine = Mesh(mesh.devices.reshape(2, 4, 4, 2, 2), ("ylo", "x", "z", "yhi", "core"))
    row = ("ylo", "x")
    col = ("z", "yhi", "core")
    return jax.shard_map(
        body,
        mesh=fine,
        in_specs=(
            P(col, row),
            P(row),
            P(row, col),
            P(row, col),
            P(col),
            P(row, None),
            P(row, None),
            P(),
            P(col, row),
            P(col, row),
            P(None, row, None),
            P(),
        ),
        out_specs=P(col, row),
        check_vma=False,
    )
```
